32 devices in a mesh: parts: 2 (over y), samp: 4 (over x, core), bond: 4 (over z).
Axes of the slice: x: 2, y: 2, z: 4, core: 2. Of those that a mesh axis runs over, the one named last changes fastest.
Arguments:
- env_start: bfloat16 [4096, 4096], P(('parts', 'samp'), 'bond'), parts along dimension 0, may hold values from -6 to 6
- stored_sites: bfloat16 [4, 4, 1024, 4, 4096], P('parts', 'samp', None, None, 'bond'), parts along dimension 0, may hold values from -1 to 1
- slab_order: int32 [4, 4], P('parts'), parts along dimension 0, may hold values from 0 to 3, each once within a row
- chosen: int32 [4096, 2], P(('parts', 'samp')), parts along dimension 0, may hold values from 0 to 3
Outputs:
- probabilities: float32 [4096, 2, 4], P(('parts', 'samp')), parts along dimension 0
- env_final: float32 [4096, 4096], P(('parts', 'samp'), 'bond'), parts along dimension 0
The draws below stay inside these ranges and needn't reach their ends.
There are 2 independent parts, one for each index of `parts`. The reference program is written for one: setup_inputs(seed, part) draws one part's arguments, and reference() takes and returns one part's arrays. A program takes and returns all parts, laid end to end along the dimension named above; each array names one. Nothing has to cross between parts.
Inputs may be any that keep to these rules, and one draw needn't show every extreme that they name: Each row of slab_order names every index of samp once.
All inputs are finite; a program needn't handle non-finite values.
Results may differ from the reference program's by a relative error of at most 0.005.
Values may be sent and summed in bfloat16 or wider, within the bound.
No kernel may reach another device: no remote copies, remote signals or barrier semaphores. Data moves between devices by JAX's collectives and lax.ppermute only.
A program may use at most 192 MiB of HBM per device.

```python
import math
import jax
import jax.numpy as jnp
from jax import lax

CHI = 4096
D_F = 4
STEPS = 2
SAMPLES = 2048
SLAB = 1024
N_SAMP = 4


def draw_stored_sites(key, part):
    key_base = jax.random.fold_in(key, 11)
    key_cols = jax.random.fold_in(key, 12)
    base = jnp.clip(jax.random.normal(key_base, (STEPS, N_SAMP, SLAB, D_F, CHI), jnp.float32), -6.0, 6.0)
    position = jnp.arange(CHI, dtype=jnp.float32) / max(CHI - 1, 1)
    col_scale = jnp.exp(jax.random.uniform(key_cols, (CHI,), jnp.float32, 0.0, math.log(10.0)))
    col_scale = col_scale * jnp.exp(0.5 * math.log(3.0) * position)
    scaled = base * col_scale / (4.0 * math.sqrt(CHI))
    return jnp.clip(scaled, -1.0, 1.0).astype(jnp.bfloat16)


def with_ends(values, own_key, least, top_value):
    dims = values.shape
    spot = [jax.random.randint(jax.random.fold_in(own_key, axis), (), 0, dims[axis]) for axis in range(len(dims))]
    values = values.at[tuple(spot)].set(least)
    longest = dims.index(max(dims))
    spot[longest] = (spot[longest] + 1) % dims[longest]
    return values.at[tuple(spot)].set(top_value)


def shard_levels(own_key, shape, cuts, smallest, top_value):
    gain, own = 1.0, jax.random.fold_in(own_key, 6)
    for axis_at, parts in cuts:
        draws = jnp.exp(jax.random.uniform(jax.random.fold_in(own, axis_at), (parts,), jnp.float32, smallest / len(cuts), top_value / len(cuts)))
        gain = gain * jnp.repeat(draws, shape[axis_at] // parts).reshape([-1 if axis == axis_at else 1 for axis in range(len(shape))])
    return gain


def gaussian(rng, extent, spread, most, pieces=(), kind=jnp.bfloat16):
    level = shard_levels(rng, extent, pieces, -0.22, 0.18) if pieces else 1.0
    drawn = jax.random.normal(rng, extent, jnp.float32) * spread * level
    return jnp.minimum(jnp.maximum(drawn, -most), most).astype(kind)


def setup_inputs(seed: int = 0, part: int = 0) -> dict:
    key_of = jax.random.split(jax.random.key(seed), 5)
    part_keys = jax.random.split(jax.random.fold_in(key_of[4], part), 5)
    return {
        "env_start": gaussian(part_keys[0], (SAMPLES, CHI), 1.0, 6.0, ((0, 4), (1, 4))),
        "stored_sites": draw_stored_sites(jax.random.fold_in(jax.random.fold_in(key_of[4], part), 71), part),
        "slab_order": jax.vmap(lambda own: jax.random.permutation(own, N_SAMP))(jax.random.split(part_keys[2], STEPS)).reshape((STEPS, N_SAMP)).astype(jnp.int32),
        "chosen": with_ends(jax.random.randint(part_keys[3], (SAMPLES, STEPS), 0, D_F), jax.random.fold_in(part_keys[3], 1), 0, D_F - 1).astype(jnp.int32),
    }


epsilon = 1e-06

def reference(env_start, stored_sites, slab_order, chosen):
    samples = env_start.shape[0]
    raw_env = env_start
    factor = jnp.ones((samples,), jnp.float32)
    outcomes = jnp.arange(D_F, dtype=jnp.int32)
    prob_list = []
    selected = None
    for site_index in range(STEPS):
        blocks = raw_env.reshape(samples, N_SAMP, SLAB)
        ordered = jnp.take(blocks, slab_order[site_index].astype(jnp.int32), axis=1).reshape(samples, CHI)
        site_block = stored_sites[site_index].reshape(CHI, D_F * CHI)
        product = jnp.dot(ordered, site_block, preferred_element_type=jnp.float32).reshape(samples, D_F, CHI)
        amplitude = product * factor[:, None, None]
        totals = lax.optimization_barrier(jnp.sum(amplitude * amplitude, axis=2))
        prob_list.append(totals / lax.optimization_barrier(jnp.sum(totals, axis=1, keepdims=True)))
        selector = (chosen[:, site_index][:, None] == outcomes[None, :]).astype(jnp.float32)
        selected = jnp.einsum('sn,snc->sc', selector, product)
        chosen_total = lax.optimization_barrier(jnp.sum(totals * selector, axis=1))
        factor = factor * lax.rsqrt(chosen_total / CHI + epsilon)
        if site_index + 1 < STEPS:
            raw_env = selected.astype(jnp.bfloat16)
    env_final = selected * factor[:, None]
    return (jnp.stack(prob_list, axis=1), env_final)
```

```python
import functools

import jax
import jax.numpy as jnp
from jax import lax
from jax.experimental import pallas as pl
from jax.experimental.pallas import tpu as pltpu
from jax.sharding import PartitionSpec as P

epsilon = 1e-06
VMEM_LIMIT = 48 * 2**20
DEDUPE = False


def divisor(extent, most):
    size = min(extent, most)
    while extent % size:
        size -= 1
    return size


def params():
    return pltpu.CompilerParams(vmem_limit_bytes=VMEM_LIMIT)


def outcome_major(stored_sites, site):
    _, _, rows, outcomes, columns = stored_sites.shape
    tile = divisor(rows, 128)

    def kernel(source, target):
        target[...] = jnp.swapaxes(source[0, 0], 0, 1)

    return pl.pallas_call(
        kernel,
        grid=(rows // tile,),
        in_specs=[pl.BlockSpec((1, 1, tile, outcomes, columns), lambda i: (site, 0, i, 0, 0))],
        out_specs=pl.BlockSpec((outcomes, tile, columns), lambda i: (0, i, 0)),
        out_shape=jax.ShapeDtypeStruct((outcomes, rows, columns), stored_sites.dtype),
        compiler_params=params(),
        cost_estimate=pl.CostEstimate(
            flops=0, bytes_accessed=4 * rows * outcomes * columns, transcendentals=0
        ),
    )(stored_sites)


def fetch(sources, code, slot_of, target, sem):
    for at, (ref, index) in enumerate(sources):

        @pl.when(code == at)
        def _(ref=ref, index=index):
            pltpu.make_async_copy(slot_of(ref, index), target, sem).start()


def candidates(refs):
    own, near, far, passed = refs
    return [(own, None), (near, None), (far, 0), (far, 1), (passed, 0), (passed, 1)]


def places_of(wanted, column):
    middle = (column == 1) | (column == 2)
    far = jnp.where(middle, 2, 4) + jnp.where((wanted == 1) | (wanted == 2), 0, 1)
    near = wanted // 2 == column // 2
    return jnp.where(wanted == column, 0, jnp.where(near, 1, far)).astype(jnp.int32)


def gather(block):
    near = lax.ppermute(block, "bond", [(0, 1), (1, 0), (2, 3), (3, 2)])
    both = jnp.stack([block, near])
    far = lax.ppermute(both, "bond", [(1, 2), (2, 1)])
    passed = lax.ppermute(far, "bond", [(0, 1), (1, 0), (2, 3), (3, 2)])
    return block, near, far, passed


def pick(blocks, places, start, rows):
    count = places.shape[0]
    columns = blocks[0].shape[1]
    scalars = jnp.concatenate([places, jnp.reshape(start, (1,)).astype(jnp.int32)])

    def kernel(scalars_ref, own, near, far, passed, target, sems):
        begin = pl.multiple_of(scalars_ref[count], 16)

        def slot_of(ref, index):
            ref = ref if index is None else ref.at[index]
            return ref.at[pl.ds(begin, rows)]

        for slot in range(count):
            fetch(
                candidates((own, near, far, passed)),
                scalars_ref[slot],
                slot_of,
                target.at[slot],
                sems.at[slot],
            )
        for slot in range(count):
            pltpu.make_async_copy(slot_of(own, None), target.at[slot], sems.at[slot]).wait()

    return pl.pallas_call(
        kernel,
        grid_spec=pltpu.PrefetchScalarGridSpec(
            num_scalar_prefetch=1,
            grid=(1,),
            in_specs=[pl.BlockSpec(memory_space=pl.ANY)] * 4,
            out_specs=pl.BlockSpec((count, rows, columns), lambda i, s: (0, 0, 0)),
            scratch_shapes=[pltpu.SemaphoreType.DMA((count,))],
        ),
        out_shape=jax.ShapeDtypeStruct((count, rows, columns), blocks[0].dtype),
        compiler_params=params(),
        cost_estimate=pl.CostEstimate(
            flops=0, bytes_accessed=4 * count * rows * columns, transcendentals=0
        ),
    )(scalars, *blocks)


def partials(blocks, places, other, slabs, column):
    count = places.shape[0]
    rows, depth = blocks[0].shape
    outcomes, _, columns = slabs[0].shape
    quarters = 4 if len(other) == 4 else 1
    if quarters == 4:
        places = jnp.concatenate([places, places_of(jnp.arange(4), column)])

    def kernel(places_ref, *refs):
        mine, refs = refs[:4], refs[4:]
        theirs, refs = refs[: len(other)], refs[len(other) :]
        weights, refs = refs[:count], refs[count:]
        own_out, other_out, left, sems = refs

        @pl.when(pl.program_id(0) == 0)
        def _():
            def block_of(ref, index):
                return ref if index is None else ref.at[index]

            for slot in range(count):
                fetch(
                    candidates(mine),
                    places_ref[slot],
                    block_of,
                    left.at[slot, pl.ds(rows, rows)],
                    sems.at[0, slot],
                )
            if quarters == 1:
                copies = [pltpu.make_async_copy(theirs[0], left.at[:, pl.ds(0, rows)], sems.at[1, 0])]
                copies[0].start()
            else:
                part = rows // quarters
                copies = []
                for q in range(quarters):
                    target = left.at[:, pl.ds(q * part, part)]
                    fetch(
                        candidates(theirs), places_ref[count + q], block_of, target, sems.at[1, q]
                    )
                    copies.append(pltpu.make_async_copy(theirs[0], target, sems.at[1, q]))
            for slot in range(count):
                pltpu.make_async_copy(
                    mine[0], left.at[slot, pl.ds(rows, rows)], sems.at[0, slot]
                ).wait()
            for copy in copies:
                copy.wait()

        total = jnp.dot(left[0], weights[0][0], preferred_element_type=jnp.float32)
        for slot in range(1, count):
            total += jnp.dot(left[slot], weights[slot][0], preferred_element_type=jnp.float32)
        other_out[0] = total[:rows].astype(other_out.dtype)
        own_out[0] = total[rows:]

    result = pl.BlockSpec((1, rows, columns), lambda n, s: (n, 0, 0))
    size = outcomes * columns
    return pl.pallas_call(
        kernel,
        grid_spec=pltpu.PrefetchScalarGridSpec(
            num_scalar_prefetch=1,
            grid=(outcomes,),
            in_specs=[pl.BlockSpec(memory_space=pl.ANY)] * (4 + len(other))
            + [pl.BlockSpec((1, depth, columns), lambda n, s: (n, 0, 0))] * count,
            out_specs=[result, result],
            scratch_shapes=[
                pltpu.VMEM((count, 2 * rows, depth), blocks[0].dtype),
                pltpu.SemaphoreType.DMA((2, 4)),
            ],
        ),
        out_shape=[
            jax.ShapeDtypeStruct((outcomes, rows, columns), jnp.float32),
            jax.ShapeDtypeStruct((outcomes, rows, columns), jnp.bfloat16),
        ],
        compiler_params=params(),
        cost_estimate=pl.CostEstimate(
            flops=4 * count * rows * depth * size,
            bytes_accessed=2 * count * depth * size + 6 * rows * size,
            transcendentals=0,
        ),
    )(places, *blocks, *other, *slabs)


def combine(own, received, chosen, kept):
    outcomes, rows, columns = own.shape
    tile = divisor(rows, 128)

    def kernel(own_ref, received_ref, chosen_ref, selected_ref, totals_ref):
        picked = chosen_ref[...]
        lanes = lax.broadcasted_iota(jnp.int32, (tile, 128), 1)
        selected = jnp.zeros((tile, columns), jnp.float32)
        squares = jnp.zeros((tile, 128), jnp.float32)
        for n in range(outcomes):
            product = own_ref[n] + received_ref[n].astype(jnp.float32)
            selected = jnp.where(picked == n, product, selected)
            norm = jnp.sum(product * product, axis=1, keepdims=True)
            squares = jnp.where(lanes == n, norm, squares)
        selected_ref[...] = selected.astype(selected_ref.dtype)
        totals_ref[...] = squares.T[:8]

    block = pl.BlockSpec((outcomes, tile, columns), lambda i: (0, i, 0))
    selected, totals = pl.pallas_call(
        kernel,
        grid=(rows // tile,),
        in_specs=[block, block, pl.BlockSpec((tile, 1), lambda i: (i, 0))],
        out_specs=[
            pl.BlockSpec((tile, columns), lambda i: (i, 0)),
            pl.BlockSpec((8, tile), lambda i: (0, i)),
        ],
        out_shape=[
            jax.ShapeDtypeStruct((rows, columns), kept),
            jax.ShapeDtypeStruct((8, rows), jnp.float32),
        ],
        compiler_params=params(),
        cost_estimate=pl.CostEstimate(
            flops=4 * outcomes * rows * columns,
            bytes_accessed=8 * outcomes * rows * columns,
            transcendentals=0,
        ),
    )(own, received, chosen)
    return selected, totals[:outcomes]


def body(env_start, stored_sites, slab_order, chosen, *, samp, bond):
    steps = stored_sites.shape[0]
    slab = stored_sites.shape[2]
    samples, width = env_start.shape
    inner = samp // 2
    mine = lax.axis_index("samp")
    half, place = mine // inner, mine % inner
    across = [(i, (i + inner) % samp) for i in range(samp)]
    column = lax.axis_index("bond")

    def inner_perm(shift):
        return [
            (h * inner + i, h * inner + (i + shift) % inner) for h in range(2) for i in range(inner)
        ]

    slabs = []
    for site in range(steps):
        block = outcome_major(stored_sites, site)
        slabs.append(
            [block] + [lax.ppermute(block, "samp", inner_perm(d)) for d in range(1, inner)]
        )

    def order_of(site, which):
        ids = [which * inner + (place - d) % inner for d in range(inner)]
        return jnp.stack([slab_order[site, i] for i in ids])

    chunks = 4
    rows = samples // chunks
    env = [env_start[c * rows : (c + 1) * rows] for c in range(chunks)]
    totals = []
    for site in range(steps):
        last = site + 1 == steps
        own_places = places_of(order_of(site, half), column)
        other_places = places_of(order_of(site, 1 - half), column)
        next_env, site_totals = [], []
        for c in range(chunks):
            blocks = gather(env[c])
            if DEDUPE:
                part = rows // bond
                sent = pick(blocks, other_places, column * part, part)
                other = gather(lax.ppermute(sent, "samp", across))
            else:
                sent = pick(blocks, other_places, 0, rows)
                other = (lax.ppermute(sent, "samp", across),)
            own_part, other_part = partials(blocks, own_places, other, slabs[site], column)
            received = lax.ppermute(other_part, "samp", across)
            selected, squares = combine(
                own_part,
                received,
                chosen[c * rows : (c + 1) * rows, site : site + 1],
                jnp.float32 if last else jnp.bfloat16,
            )
            next_env.append(selected)
            site_totals.append(squares)
        env = next_env
        totals.append(jnp.concatenate(site_totals, axis=1))

    stacked = jnp.stack(totals)
    summed = stacked
    for d in range(1, bond):
        summed = summed + lax.ppermute(stacked, "bond", [(i, (i + d) % bond) for i in range(bond)])
    outcomes = jnp.arange(stored_sites.shape[3], dtype=jnp.int32)
    factor = jnp.ones((1, samples), jnp.float32)
    probabilities = []
    for site in range(steps):
        scaled = summed[site] * (factor * factor)
        probabilities.append(scaled / jnp.sum(scaled, axis=0, keepdims=True))
        selector = chosen[:, site][None, :] == outcomes[:, None]
        chosen_total = jnp.sum(jnp.where(selector, scaled, 0.0), axis=0, keepdims=True)
        factor = factor * lax.rsqrt(chosen_total / (width * bond) + epsilon)
    env_final = jnp.concatenate(env, axis=0) * factor[0][:, None]
    return jnp.stack(probabilities).transpose(2, 0, 1), env_final


def plain_body(env_start, stored_sites, slab_order, chosen):
    samples = env_start.shape[0]
    steps = stored_sites.shape[0]
    slab = stored_sites.shape[2]
    outcomes = jnp.arange(stored_sites.shape[3], dtype=jnp.int32)
    gathered = lax.all_gather(env_start, "bond", axis=1, tiled=True)
    bond_width = gathered.shape[1]
    factor = jnp.ones((samples,), jnp.float32)
    prob_list, raw_totals, selectors = [], [], []
    selected = None
    for site in range(steps):
        ordered = jnp.concatenate(
            [
                lax.dynamic_slice_in_dim(gathered, slab_order[site, i] * slab, slab, axis=1)
                for i in range(slab_order.shape[1])
            ],
            axis=1,
        )
        portion = lax.all_gather(stored_sites[site], "samp", axis=0, tiled=True)
        product = jnp.dot(
            ordered, portion.reshape(bond_width, -1), preferred_element_type=jnp.float32
        )
        product = lax.optimization_barrier(product)
        product = product.reshape(samples, stored_sites.shape[3], stored_sites.shape[4])
        selector = (chosen[:, site][:, None] == outcomes[None, :]).astype(jnp.float32)
        selected = jnp.sum(selector[:, :, None] * product, axis=1)
        raw_totals.append(jnp.sum(product * product, axis=2))
        selectors.append(selector)
        if site + 1 < steps:
            gathered = lax.all_gather(selected.astype(jnp.bfloat16), "bond", axis=1, tiled=True)
    reduced = lax.psum(tuple(raw_totals), "bond")
    for site in range(steps):
        totals = reduced[site] * (factor * factor)[:, None]
        prob_list.append(totals / jnp.sum(totals, axis=1, keepdims=True))
        chosen_total = jnp.sum(totals * selectors[site], axis=1)
        factor = factor * lax.rsqrt(chosen_total / bond_width + epsilon)
    return jnp.stack(prob_list, axis=1), selected * factor[:, None]


def solution(mesh):
    samp, bond = mesh.shape["samp"], mesh.shape["bond"]

    def choose(env_start, stored_sites, slab_order, chosen):
        if stored_sites.shape[2] == env_start.shape[1] and samp == 4 and bond == 4:
            return body(env_start, stored_sites, slab_order, chosen, samp=samp, bond=bond)
        return plain_body(env_start, stored_sites, slab_order, chosen)

    return jax.shard_map(
        choose,
        mesh=mesh,
        in_specs=(
            P(("parts", "samp"), "bond"),
            P("parts", "samp", None, None, "bond"),
            P("parts", None),
            P(("parts", "samp"), None),
        ),
        out_specs=(P(("parts", "samp"), None, None), P(("parts", "samp"), "bond")),
        check_vma=False,
    )
```

```python
import functools

import jax
import jax.numpy as jnp
from jax import lax
from jax.experimental import pallas as pl
from jax.experimental.pallas import tpu as pltpu
from jax.sharding import PartitionSpec as P

epsilon = 1e-06
VMEM_LIMIT = 48 * 2**20
COST = 10.0
CHUNKS = 4


def divisor(extent, most):
    size = min(extent, most)
    while extent % size:
        size -= 1
    return size


def params():
    return pltpu.CompilerParams(vmem_limit_bytes=VMEM_LIMIT)


ANY = pl.BlockSpec(memory_space=pl.ANY)


def cost(flops, moved):
    return pl.CostEstimate(
        flops=int(COST * flops), bytes_accessed=int(COST * moved), transcendentals=0
    )


def outcome_major(stored_sites, site, after=()):
    _, _, rows, outcomes, columns = stored_sites.shape
    tile = divisor(rows, 128)

    def kernel(source, *refs):
        refs[-1][...] = jnp.swapaxes(source[0, 0], 0, 1)

    return pl.pallas_call(
        kernel,
        grid=(rows // tile,),
        in_specs=[pl.BlockSpec((1, 1, tile, outcomes, columns), lambda i: (site, 0, i, 0, 0))]
        + [ANY] * len(after),
        out_specs=pl.BlockSpec((outcomes, tile, columns), lambda i: (0, i, 0)),
        out_shape=jax.ShapeDtypeStruct((outcomes, rows, columns), stored_sites.dtype),
        compiler_params=params(),
        cost_estimate=cost(0, 8 * rows * outcomes * columns),
    )(stored_sites, *after)


def fetch(sources, code, view, target, sem):
    for at, ref in enumerate(sources):

        @pl.when(code == at)
        def _(ref=ref):
            pltpu.make_async_copy(view(ref), target, sem).start()


def gather(block, bond):
    return [block] + [
        lax.ppermute(block, "bond", [(i, (i + d) % bond) for i in range(bond)])
        for d in range(1, bond)
    ]


def pick(blocks, places, start, rows, after=()):
    count = places.shape[0]
    columns = blocks[0].shape[1]
    scalars = jnp.concatenate([places, jnp.reshape(start, (1,)).astype(jnp.int32)])

    def kernel(scalars_ref, *refs):
        sources = refs[: len(blocks)]
        target, sems = refs[-2:]
        begin = pl.multiple_of(scalars_ref[count], 16)

        def view(ref):
            return ref.at[pl.ds(begin, rows)]

        for slot in range(count):
            fetch(sources, scalars_ref[slot], view, target.at[slot], sems.at[slot])
        for slot in range(count):
            pltpu.make_async_copy(view(sources[0]), target.at[slot], sems.at[slot]).wait()

    return pl.pallas_call(
        kernel,
        grid_spec=pltpu.PrefetchScalarGridSpec(
            num_scalar_prefetch=1,
            grid=(1,),
            in_specs=[ANY] * (len(blocks) + len(after)),
            out_specs=pl.BlockSpec((count, rows, columns), lambda i, s: (0, 0, 0)),
            scratch_shapes=[pltpu.SemaphoreType.DMA((count,))],
        ),
        out_shape=jax.ShapeDtypeStruct((count, rows, columns), blocks[0].dtype),
        compiler_params=params(),
        cost_estimate=cost(0, 4 * count * rows * columns),
    )(scalars, *blocks, *after)


def partials(blocks, places, other, slabs, after=()):
    count = len(slabs)
    rows, depth = blocks[0].shape
    outcomes, _, columns = slabs[0].shape
    runs = len(other)
    part = rows // runs

    def kernel(places_ref, *refs):
        mine, refs = refs[: len(blocks)], refs[len(blocks) :]
        theirs, refs = refs[:runs], refs[runs:]
        weights, refs = refs[:count], refs[count:]
        own_out, other_out, left, sems = refs[-4:]

        @pl.when(pl.program_id(0) == 0)
        def _():
            def whole(ref):
                return ref

            def upper(slot):
                return left.at[slot, pl.ds(rows, rows)]

            def lower(run):
                return left.at[:, pl.ds(run * part, part)]

            for slot in range(count):
                fetch(mine, places_ref[slot], whole, upper(slot), sems.at[0, slot])
            for run in range(runs):
                fetch(theirs, places_ref[count + run], whole, lower(run), sems.at[1, run])
            for slot in range(count):
                pltpu.make_async_copy(mine[0], upper(slot), sems.at[0, slot]).wait()
            for run in range(runs):
                pltpu.make_async_copy(theirs[0], lower(run), sems.at[1, run]).wait()

        total = jnp.dot(left[0], weights[0][0], preferred_element_type=jnp.float32)
        for slot in range(1, count):
            total += jnp.dot(left[slot], weights[slot][0], preferred_element_type=jnp.float32)
        other_out[0] = total[:rows].astype(other_out.dtype)
        own_out[0] = total[rows:]

    result = pl.BlockSpec((1, rows, columns), lambda n, s: (n, 0, 0))
    size = outcomes * columns
    return pl.pallas_call(
        kernel,
        grid_spec=pltpu.PrefetchScalarGridSpec(
            num_scalar_prefetch=1,
            grid=(outcomes,),
            in_specs=[ANY] * (len(blocks) + runs)
            + [pl.BlockSpec((1, depth, columns), lambda n, s: (n, 0, 0))] * count
            + [ANY] * len(after),
            out_specs=[result, result],
            scratch_shapes=[
                pltpu.VMEM((count, 2 * rows, depth), blocks[0].dtype),
                pltpu.SemaphoreType.DMA((2, max(count, runs))),
            ],
        ),
        out_shape=[
            jax.ShapeDtypeStruct((outcomes, rows, columns), jnp.float32),
            jax.ShapeDtypeStruct((outcomes, rows, columns), jnp.bfloat16),
        ],
        compiler_params=params(),
        cost_estimate=cost(
            8 * count * rows * depth * size, 2 * count * depth * size + 6 * rows * size
        ),
    )(places, *blocks, *other, *slabs, *after)


def combine(own, received, chosen, kept, after=()):
    outcomes, rows, columns = own.shape
    tile = divisor(rows, 128)

    def kernel(own_ref, received_ref, chosen_ref, *refs):
        selected_ref, totals_ref = refs[-2:]
        picked = chosen_ref[...]
        lanes = lax.broadcasted_iota(jnp.int32, (tile, 128), 1)
        selected = jnp.zeros((tile, columns), jnp.float32)
        squares = jnp.zeros((tile, 128), jnp.float32)
        for n in range(outcomes):
            product = own_ref[n] + received_ref[n].astype(jnp.float32)
            selected = jnp.where(picked == n, product, selected)
            norm = jnp.sum(product * product, axis=1, keepdims=True)
            squares = jnp.where(lanes == n, norm, squares)
        selected_ref[...] = selected.astype(selected_ref.dtype)
        totals_ref[...] = squares.T[:8]

    block = pl.BlockSpec((outcomes, tile, columns), lambda i: (0, i, 0))
    selected, totals = pl.pallas_call(
        kernel,
        grid=(rows // tile,),
        in_specs=[block, block, pl.BlockSpec((tile, 1), lambda i: (i, 0))] + [ANY] * len(after),
        out_specs=[
            pl.BlockSpec((tile, columns), lambda i: (i, 0)),
            pl.BlockSpec((8, tile), lambda i: (0, i)),
        ],
        out_shape=[
            jax.ShapeDtypeStruct((rows, columns), kept),
            jax.ShapeDtypeStruct((8, rows), jnp.float32),
        ],
        compiler_params=params(),
        cost_estimate=cost(4 * outcomes * rows * columns, 8 * outcomes * rows * columns),
    )(own, received, chosen, *after)
    return selected, totals[:outcomes]


def body(env_start, stored_sites, slab_order, chosen, *, samp, bond):
    steps = stored_sites.shape[0]
    samples, width = env_start.shape
    inner = samp // 2
    mine = lax.axis_index("samp")
    half, place = mine // inner, mine % inner
    across = [(i, (i + inner) % samp) for i in range(samp)]
    column = lax.axis_index("bond")
    beside = [(i, i ^ 1) for i in range(bond)]

    def share(block):
        return [block] + [
            lax.ppermute(
                block,
                "samp",
                [(h * inner + i, h * inner + (i + d) % inner) for h in range(2) for i in range(inner)],
            )
            for d in range(1, inner)
        ]

    def places_of(site, which):
        ids = jnp.stack(
            [slab_order[site, which * inner + (place - d) % inner] for d in range(inner)]
        )
        return ((column - ids) % bond).astype(jnp.int32)

    side = column % 2
    runs = jnp.stack([side, 1 - side]).astype(jnp.int32)
    own_places = [jnp.concatenate([places_of(k, half), runs]) for k in range(steps)]
    other_places = [places_of(k, 1 - half) for k in range(steps)]

    chunks = CHUNKS
    rows = samples // chunks
    count = steps * chunks
    slabs = {0: share(outcome_major(stored_sites, 0))}
    env = {j: env_start[j * rows : (j + 1) * rows] for j in range(chunks)}
    blocks, halves, parts, received, outs = {}, {}, {}, {}, {}
    order = []

    def latest():
        return order[-1:]

    def start_gather(j):
        if 0 <= j < count:
            source = env[j] if j < chunks else outs[j - chunks][0]
            if j < chunks and order:
                source, _ = lax.optimization_barrier((source, order[-1]))
            blocks[j] = gather(source, bond)

    def start_cross(j):
        if 0 <= j < count:
            part = rows // 2
            sent = pick(blocks[j], other_places[j // chunks], side * part, part, latest())
            order.append(sent)
            halves[j] = [lax.ppermute(sent, "samp", across)]

    def start_swap(j):
        if 0 <= j < count:
            halves[j].append(lax.ppermute(halves[j][0], "bond", beside))

    def multiply(j):
        if 0 <= j < count:
            parts[j], sent = partials(
                blocks[j], own_places[j // chunks], halves[j], slabs[j // chunks], latest()
            )
            order.append(sent)
            received[j] = lax.ppermute(sent, "samp", across)

    def finish(j):
        if 0 <= j < count:
            site, c = j // chunks, j % chunks
            outs[j] = combine(
                parts[j],
                received[j],
                chosen[c * rows : (c + 1) * rows, site : site + 1],
                jnp.float32 if site + 1 == steps else jnp.bfloat16,
                latest(),
            )
            order.append(outs[j][0])

    def relay(k):
        if k < steps:
            slabs[k] = share(outcome_major(stored_sites, k, latest()))
            order.append(slabs[k][0])

    start_gather(0)
    start_cross(0)
    start_gather(1)
    start_swap(0)
    multiply(0)
    start_cross(1)
    start_gather(2)
    start_swap(1)
    start_cross(2)
    start_gather(3)
    for tick in range(1, count + 1):
        if tick > 1:
            finish(tick - 2)
            start_gather(tick + 2)
            start_cross(tick + 1)
        multiply(tick)
        relay(tick)
        start_swap(tick + 1)
    finish(count - 1)

    env = [outs[(steps - 1) * chunks + c][0] for c in range(chunks)]
    stacked = jnp.stack(
        [
            jnp.concatenate([outs[k * chunks + c][1] for c in range(chunks)], axis=1)
            for k in range(steps)
        ]
    )
    summed = stacked
    for d in range(1, bond):
        summed = summed + lax.ppermute(stacked, "bond", [(i, (i + d) % bond) for i in range(bond)])
    outcomes = jnp.arange(stored_sites.shape[3], dtype=jnp.int32)
    factor = jnp.ones((1, samples), jnp.float32)
    probabilities = []
    for site in range(steps):
        scaled = summed[site] * (factor * factor)
        probabilities.append(scaled / jnp.sum(scaled, axis=0, keepdims=True))
        selector = chosen[:, site][None, :] == outcomes[:, None]
        chosen_total = jnp.sum(jnp.where(selector, scaled, 0.0), axis=0, keepdims=True)
        factor = factor * lax.rsqrt(chosen_total / (width * bond) + epsilon)
    env_final = jnp.concatenate(env, axis=0) * factor[0][:, None]
    return jnp.stack(probabilities).transpose(2, 0, 1), env_final


def plain_body(env_start, stored_sites, slab_order, chosen):
    samples = env_start.shape[0]
    steps = stored_sites.shape[0]
    slab = stored_sites.shape[2]
    outcomes = jnp.arange(stored_sites.shape[3], dtype=jnp.int32)
    gathered = lax.all_gather(env_start, "bond", axis=1, tiled=True)
    bond_width = gathered.shape[1]
    factor = jnp.ones((samples,), jnp.float32)
    prob_list, raw_totals, selectors = [], [], []
    selected = None
    for site in range(steps):
        ordered = jnp.concatenate(
            [
                lax.dynamic_slice_in_dim(gathered, slab_order[site, i] * slab, slab, axis=1)
                for i in range(slab_order.shape[1])
            ],
            axis=1,
        )
        portion = lax.all_gather(stored_sites[site], "samp", axis=0, tiled=True)
        product = jnp.dot(
            ordered, portion.reshape(bond_width, -1), preferred_element_type=jnp.float32
        )
        product = lax.optimization_barrier(product)
        product = product.reshape(samples, stored_sites.shape[3], stored_sites.shape[4])
        selector = (chosen[:, site][:, None] == outcomes[None, :]).astype(jnp.float32)
        selected = jnp.sum(selector[:, :, None] * product, axis=1)
        raw_totals.append(jnp.sum(product * product, axis=2))
        selectors.append(selector)
        if site + 1 < steps:
            gathered = lax.all_gather(selected.astype(jnp.bfloat16), "bond", axis=1, tiled=True)
    reduced = lax.psum(tuple(raw_totals), "bond")
    for site in range(steps):
        totals = reduced[site] * (factor * factor)[:, None]
        prob_list.append(totals / jnp.sum(totals, axis=1, keepdims=True))
        chosen_total = jnp.sum(totals * selectors[site], axis=1)
        factor = factor * lax.rsqrt(chosen_total / bond_width + epsilon)
    return jnp.stack(prob_list, axis=1), selected * factor[:, None]


def solution(mesh):
    samp, bond = mesh.shape["samp"], mesh.shape["bond"]

    def choose(env_start, stored_sites, slab_order, chosen):
        if stored_sites.shape[2] == env_start.shape[1] and samp == 4 and bond == 4:
            return body(env_start, stored_sites, slab_order, chosen, samp=samp, bond=bond)
        return plain_body(env_start, stored_sites, slab_order, chosen)

    return jax.shard_map(
        choose,
        mesh=mesh,
        in_specs=(
            P(("parts", "samp"), "bond"),
            P("parts", "samp", None, None, "bond"),
            P("parts", None),
            P(("parts", "samp"), None),
        ),
        out_specs=(P(("parts", "samp"), None, None), P(("parts", "samp"), "bond")),
        check_vma=False,
    )
```

```python
import functools

import jax
import jax.numpy as jnp
from jax import lax
from jax.experimental import pallas as pl
from jax.experimental.pallas import tpu as pltpu
from jax.sharding import PartitionSpec as P

epsilon = 1e-06
VMEM_LIMIT = 48 * 2**20
COST = 10.0
CHUNKS = 4


def divisor(extent, most):
    size = min(extent, most)
    while extent % size:
        size -= 1
    return size


def params():
    return pltpu.CompilerParams(vmem_limit_bytes=VMEM_LIMIT)


ANY = pl.BlockSpec(memory_space=pl.ANY)


def cost(flops, moved):
    return pl.CostEstimate(
        flops=int(COST * flops), bytes_accessed=int(COST * moved), transcendentals=0
    )


def outcome_major(stored_sites, site, after=()):
    _, _, rows, outcomes, columns = stored_sites.shape
    tile = divisor(rows, 128)

    def kernel(source, *refs):
        refs[-1][...] = jnp.swapaxes(source[0, 0], 0, 1)

    return pl.pallas_call(
        kernel,
        grid=(rows // tile,),
        in_specs=[pl.BlockSpec((1, 1, tile, outcomes, columns), lambda i: (site, 0, i, 0, 0))]
        + [ANY] * len(after),
        out_specs=pl.BlockSpec((outcomes, tile, columns), lambda i: (0, i, 0)),
        out_shape=jax.ShapeDtypeStruct((outcomes, rows, columns), stored_sites.dtype),
        compiler_params=params(),
        cost_estimate=cost(0, 8 * rows * outcomes * columns),
    )(stored_sites, *after)


def fetch(sources, code, view, target, sem):
    for at, ref in enumerate(sources):

        @pl.when(code == at)
        def _(ref=ref):
            pltpu.make_async_copy(view(ref), target, sem).start()


def gather(block, bond):
    return [block] + [
        lax.ppermute(block, "bond", [(i, (i + d) % bond) for i in range(bond)])
        for d in range(1, bond)
    ]


def pick(blocks, places, start, rows, after=()):
    count = places.shape[0]
    columns = blocks[0].shape[1]
    scalars = jnp.concatenate([places, jnp.reshape(start, (1,)).astype(jnp.int32)])

    def kernel(scalars_ref, *refs):
        sources = refs[: len(blocks)]
        target, sems = refs[-2:]
        begin = pl.multiple_of(scalars_ref[count], 16)

        def view(ref):
            return ref.at[pl.ds(begin, rows)]

        for slot in range(count):
            fetch(sources, scalars_ref[slot], view, target.at[slot], sems.at[slot])
        for slot in range(count):
            pltpu.make_async_copy(view(sources[0]), target.at[slot], sems.at[slot]).wait()

    return pl.pallas_call(
        kernel,
        grid_spec=pltpu.PrefetchScalarGridSpec(
            num_scalar_prefetch=1,
            grid=(1,),
            in_specs=[ANY] * (len(blocks) + len(after)),
            out_specs=pl.BlockSpec((count, rows, columns), lambda i, s: (0, 0, 0)),
            scratch_shapes=[pltpu.SemaphoreType.DMA((count,))],
        ),
        out_shape=jax.ShapeDtypeStruct((count, rows, columns), blocks[0].dtype),
        compiler_params=params(),
        cost_estimate=cost(0, 4 * count * rows * columns),
    )(scalars, *blocks, *after)


def partials(blocks, places, other, slabs, after=()):
    count = len(slabs)
    rows, depth = blocks[0].shape
    outcomes, _, columns = slabs[0].shape
    runs = len(other)
    part = rows // runs

    def kernel(places_ref, *refs):
        mine, refs = refs[: len(blocks)], refs[len(blocks) :]
        theirs, refs = refs[:runs], refs[runs:]
        weights, refs = refs[:count], refs[count:]
        own_out, other_out, left, sems = refs[-4:]

        @pl.when(pl.program_id(0) == 0)
        def _():
            def whole(ref):
                return ref

            def upper(slot):
                return left.at[slot, pl.ds(rows, rows)]

            def lower(run):
                return left.at[:, pl.ds(run * part, part)]

            for slot in range(count):
                fetch(mine, places_ref[slot], whole, upper(slot), sems.at[0, slot])
            for run in range(runs):
                fetch(theirs, places_ref[count + run], whole, lower(run), sems.at[1, run])
            for slot in range(count):
                pltpu.make_async_copy(mine[0], upper(slot), sems.at[0, slot]).wait()
            for run in range(runs):
                pltpu.make_async_copy(theirs[0], lower(run), sems.at[1, run]).wait()

        total = jnp.dot(left[0], weights[0][0], preferred_element_type=jnp.float32)
        for slot in range(1, count):
            total += jnp.dot(left[slot], weights[slot][0], preferred_element_type=jnp.float32)
        other_out[0] = total[:rows].astype(other_out.dtype)
        own_out[0] = total[rows:]

    result = pl.BlockSpec((1, rows, columns), lambda n, s: (n, 0, 0))
    size = outcomes * columns
    return pl.pallas_call(
        kernel,
        grid_spec=pltpu.PrefetchScalarGridSpec(
            num_scalar_prefetch=1,
            grid=(outcomes,),
            in_specs=[ANY] * (len(blocks) + runs)
            + [pl.BlockSpec((1, depth, columns), lambda n, s: (n, 0, 0))] * count
            + [ANY] * len(after),
            out_specs=[result, result],
            scratch_shapes=[
                pltpu.VMEM((count, 2 * rows, depth), blocks[0].dtype),
                pltpu.SemaphoreType.DMA((2, max(count, runs))),
            ],
        ),
        out_shape=[
            jax.ShapeDtypeStruct((outcomes, rows, columns), jnp.float32),
            jax.ShapeDtypeStruct((outcomes, rows, columns), jnp.bfloat16),
        ],
        compiler_params=params(),
        cost_estimate=cost(
            8 * count * rows * depth * size, 2 * count * depth * size + 6 * rows * size
        ),
    )(places, *blocks, *other, *slabs, *after)


def combine(own, received, chosen, kept, after=()):
    outcomes, rows, columns = own.shape
    tile = divisor(rows, 128)

    def kernel(own_ref, received_ref, chosen_ref, *refs):
        selected_ref, totals_ref = refs[-2:]
        picked = chosen_ref[...]
        lanes = lax.broadcasted_iota(jnp.int32, (tile, 128), 1)
        selected = jnp.zeros((tile, columns), jnp.float32)
        squares = jnp.zeros((tile, 128), jnp.float32)
        for n in range(outcomes):
            product = own_ref[n] + received_ref[n].astype(jnp.float32)
            selected = jnp.where(picked == n, product, selected)
            norm = jnp.sum(product * product, axis=1, keepdims=True)
            squares = jnp.where(lanes == n, norm, squares)
        selected_ref[...] = selected.astype(selected_ref.dtype)
        totals_ref[...] = squares.T[:8]

    block = pl.BlockSpec((outcomes, tile, columns), lambda i: (0, i, 0))
    selected, totals = pl.pallas_call(
        kernel,
        grid=(rows // tile,),
        in_specs=[block, block, pl.BlockSpec((tile, 1), lambda i: (i, 0))] + [ANY] * len(after),
        out_specs=[
            pl.BlockSpec((tile, columns), lambda i: (i, 0)),
            pl.BlockSpec((8, tile), lambda i: (0, i)),
        ],
        out_shape=[
            jax.ShapeDtypeStruct((rows, columns), kept),
            jax.ShapeDtypeStruct((8, rows), jnp.float32),
        ],
        compiler_params=params(),
        cost_estimate=cost(4 * outcomes * rows * columns, 8 * outcomes * rows * columns),
    )(own, received, chosen, *after)
    return selected, totals[:outcomes]


def body(env_start, stored_sites, slab_order, chosen, *, samp, bond):
    steps = stored_sites.shape[0]
    samples, width = env_start.shape
    inner = samp // 2
    mine = lax.axis_index("samp")
    half, place = mine // inner, mine % inner
    across = [(i, (i + inner) % samp) for i in range(samp)]
    column = lax.axis_index("bond")
    beside = [(i, i ^ 1) for i in range(bond)]

    def share(block):
        return [block] + [
            lax.ppermute(
                block,
                "samp",
                [(h * inner + i, h * inner + (i + d) % inner) for h in range(2) for i in range(inner)],
            )
            for d in range(1, inner)
        ]

    def places_of(site, which):
        ids = jnp.stack(
            [slab_order[site, which * inner + (place - d) % inner] for d in range(inner)]
        )
        return ((column - ids) % bond).astype(jnp.int32)

    side = column % 2
    runs = jnp.stack([side, 1 - side]).astype(jnp.int32)
    own_places = [jnp.concatenate([places_of(k, half), runs]) for k in range(steps)]
    other_places = [places_of(k, 1 - half) for k in range(steps)]

    chunks = CHUNKS
    rows = samples // chunks
    count = steps * chunks
    slabs = {0: share(outcome_major(stored_sites, 0))}
    env = {j: env_start[j * rows : (j + 1) * rows] for j in range(chunks)}
    blocks, halves, parts, received, outs = {}, {}, {}, {}, {}
    order = []

    def latest():
        return order[-1:]

    def start_gather(j):
        if 0 <= j < count:
            source = env[j] if j < chunks else outs[j - chunks][0]
            if j < chunks and order:
                source, _ = lax.optimization_barrier((source, order[-1]))
            blocks[j] = gather(source, bond)

    def start_cross(j):
        if 0 <= j < count:
            part = rows // 2
            sent = pick(blocks[j], other_places[j // chunks], side * part, part, latest())
            order.append(sent)
            halves[j] = [lax.ppermute(sent, "samp", across)]

    def start_swap(j):
        if 0 <= j < count:
            halves[j].append(lax.ppermute(halves[j][0], "bond", beside))

    def multiply(j):
        if 0 <= j < count:
            parts[j], sent = partials(
                blocks[j], own_places[j // chunks], halves[j], slabs[j // chunks], latest()
            )
            order.append(sent)
            received[j] = lax.ppermute(sent, "samp", across)

    def finish(j):
        if 0 <= j < count:
            site, c = j // chunks, j % chunks
            outs[j] = combine(
                parts[j],
                received[j],
                chosen[c * rows : (c + 1) * rows, site : site + 1],
                jnp.float32 if site + 1 == steps else jnp.bfloat16,
                latest(),
            )
            order.append(outs[j][0])

    def relay(k):
        if k < steps:
            slabs[k] = share(outcome_major(stored_sites, k, latest()))
            order.append(slabs[k][0])

    start_gather(0)
    start_cross(0)
    start_gather(1)
    start_swap(0)
    multiply(0)
    start_cross(1)
    start_gather(2)
    start_swap(1)
    start_cross(2)
    start_gather(3)
    for tick in range(1, count + 1):
        if tick > 1:
            finish(tick - 2)
            start_gather(tick + 2)
            start_cross(tick + 1)
        multiply(tick)
        if tick > 1:
            relay(tick - 1)
        start_swap(tick + 1)
    finish(count - 1)

    env = [outs[(steps - 1) * chunks + c][0] for c in range(chunks)]
    stacked = jnp.stack(
        [
            jnp.concatenate([outs[k * chunks + c][1] for c in range(chunks)], axis=1)
            for k in range(steps)
        ]
    )
    summed = stacked
    for d in range(1, bond):
        summed = summed + lax.ppermute(stacked, "bond", [(i, (i + d) % bond) for i in range(bond)])
    outcomes = jnp.arange(stored_sites.shape[3], dtype=jnp.int32)
    factor = jnp.ones((1, samples), jnp.float32)
    probabilities = []
    for site in range(steps):
        scaled = summed[site] * (factor * factor)
        probabilities.append(scaled / jnp.sum(scaled, axis=0, keepdims=True))
        selector = chosen[:, site][None, :] == outcomes[:, None]
        chosen_total = jnp.sum(jnp.where(selector, scaled, 0.0), axis=0, keepdims=True)
        factor = factor * lax.rsqrt(chosen_total / (width * bond) + epsilon)
    env_final = jnp.concatenate(env, axis=0) * factor[0][:, None]
    return jnp.stack(probabilities).transpose(2, 0, 1), env_final


def plain_body(env_start, stored_sites, slab_order, chosen):
    samples = env_start.shape[0]
    steps = stored_sites.shape[0]
    slab = stored_sites.shape[2]
    outcomes = jnp.arange(stored_sites.shape[3], dtype=jnp.int32)
    gathered = lax.all_gather(env_start, "bond", axis=1, tiled=True)
    bond_width = gathered.shape[1]
    factor = jnp.ones((samples,), jnp.float32)
    prob_list, raw_totals, selectors = [], [], []
    selected = None
    for site in range(steps):
        ordered = jnp.concatenate(
            [
                lax.dynamic_slice_in_dim(gathered, slab_order[site, i] * slab, slab, axis=1)
                for i in range(slab_order.shape[1])
            ],
            axis=1,
        )
        portion = lax.all_gather(stored_sites[site], "samp", axis=0, tiled=True)
        product = jnp.dot(
            ordered, portion.reshape(bond_width, -1), preferred_element_type=jnp.float32
        )
        product = lax.optimization_barrier(product)
        product = product.reshape(samples, stored_sites.shape[3], stored_sites.shape[4])
        selector = (chosen[:, site][:, None] == outcomes[None, :]).astype(jnp.float32)
        selected = jnp.sum(selector[:, :, None] * product, axis=1)
        raw_totals.append(jnp.sum(product * product, axis=2))
        selectors.append(selector)
        if site + 1 < steps:
            gathered = lax.all_gather(selected.astype(jnp.bfloat16), "bond", axis=1, tiled=True)
    reduced = lax.psum(tuple(raw_totals), "bond")
    for site in range(steps):
        totals = reduced[site] * (factor * factor)[:, None]
        prob_list.append(totals / jnp.sum(totals, axis=1, keepdims=True))
        chosen_total = jnp.sum(totals * selectors[site], axis=1)
        factor = factor * lax.rsqrt(chosen_total / bond_width + epsilon)
    return jnp.stack(prob_list, axis=1), selected * factor[:, None]


def solution(mesh):
    samp, bond = mesh.shape["samp"], mesh.shape["bond"]

    def choose(env_start, stored_sites, slab_order, chosen):
        if stored_sites.shape[2] == env_start.shape[1] and samp == 4 and bond == 4:
            return body(env_start, stored_sites, slab_order, chosen, samp=samp, bond=bond)
        return plain_body(env_start, stored_sites, slab_order, chosen)

    return jax.shard_map(
        choose,
        mesh=mesh,
        in_specs=(
            P(("parts", "samp"), "bond"),
            P("parts", "samp", None, None, "bond"),
            P("parts", None),
            P(("parts", "samp"), None),
        ),
        out_specs=(P(("parts", "samp"), None, None), P(("parts", "samp"), "bond")),
        check_vma=False,
    )
```
